32 devices in a mesh: groups: 2 (over x), leaf: 16 (over z, y, core).
Axes of the slice: x: 2, y: 2, z: 4, core: 2. Of those that a mesh axis runs over, the one named last changes fastest.
Arguments:
- points: bfloat16 [8, 131072], P(None, ('groups', 'leaf')), parts along dimension 1, may hold values from -3.5 to 3.5
- weights: bfloat16 [64, 131072], P(None, ('groups', 'leaf')), parts along dimension 1, may hold values from -6 to 6
- interpolation: bfloat16 [256, 512, 256], P(('groups', 'leaf')), parts along dimension 0, may hold values from -0.25 to 0.25
- skeleton: int32 [256, 256], P(('groups', 'leaf')), parts along dimension 0, may hold values from 0 to 511, as said below
- near_lists: int32 [256, 8], P(('groups', 'leaf')), parts along dimension 0, may hold values from 0 to 127, as said below
- far_lists: int32 [256, 12], P(('groups', 'leaf')), parts along dimension 0, may hold values from 0 to 127, as said below
Outputs:
- kernel_product: float32 [64, 131072], P(None, ('groups', 'leaf')), parts along dimension 1
- derivative_product: float32 [64, 131072], P(None, ('groups', 'leaf')), parts along dimension 1
The draws below stay inside these ranges and needn't reach their ends.
There are 2 independent parts, one for each index of `groups`. The reference program is written for one: setup_inputs(seed, part) draws one part's arguments, and reference() takes and returns one part's arrays. A program takes and returns all parts, laid end to end along the dimension named above; each array names one. Nothing has to cross between parts.
Inputs may be any that keep to these rules, and one draw needn't show every extreme that they name: `skeleton`: each row holds 256 distinct positions. near_lists[j] begins with j and holds 8 distinct leaves, all within 8 leaves of j. Leaf j lies on device j // 8. far_lists[j] holds 12 distinct leaves, none on the device of leaf j or on the devices next to it; the far lists of one device's 8 leaves name at most 8 leaves of any one device, and exactly 8 of some device.
All inputs are finite; a program needn't handle non-finite values.
Results may differ from the reference program's by a relative error of at most 0.0036.
Values may be sent and summed in bfloat16 or wider, within the bound.
A program may use at most 128 MiB of HBM per device.

```python
import jax
import jax.numpy as jnp
from jax import lax

DIM = 8
RHS = 64
RANK = 256
LEAF = 512
NB = 8
FAR = 12
LEAF_DEV = 8
LEAVES = 128
POINTS = 65536
CAP = 8


def draw_points(key, part):
    key = jax.random.fold_in(key, 11)
    key_speed, key_angle, key_jitter = jax.random.split(key, 3)
    leaf_of = (jnp.arange(LEAVES * LEAF) // LEAF).astype(jnp.float32)
    frequency = jax.random.uniform(key_speed, (DIM, 1), jnp.float32, 2.0, 6.0) * (3.14159265 / LEAVES)
    offset_angle = jax.random.uniform(key_angle, (DIM, 1), jnp.float32, -3.14159265, 3.14159265)
    centre = 0.3 * jnp.sin(frequency * leaf_of[None, :] + offset_angle)
    jitter = jnp.clip(1.2 * jax.random.normal(key_jitter, (DIM, LEAVES * LEAF), jnp.float32), -3.0, 3.0)
    return (centre + jitter).astype(jnp.bfloat16)


def draw_skeleton(key, part):
    key = jax.random.fold_in(key, 23)
    leaf_keys = jax.random.split(key, LEAVES)
    return jax.vmap(lambda single: jax.random.permutation(single, LEAF)[:RANK])(leaf_keys).astype(jnp.int32)


def draw_near_lists(key, part):
    key = jax.random.fold_in(key, 37)
    span_count = 2 * LEAF_DEV
    shifts = jnp.concatenate([jnp.arange(-LEAF_DEV, 0), jnp.arange(1, LEAF_DEV + 1)]).astype(jnp.int32)
    leaf_ids = jnp.arange(LEAVES, dtype=jnp.int32)
    targets = leaf_ids[:, None] + shifts[None, :]
    inside = (targets >= 0) & (targets < LEAVES)
    scores = jax.random.randint(key, (LEAVES, span_count), 0, 2 ** 20) * span_count + jnp.arange(span_count)[None, :]
    scores = jnp.where(inside, scores, scores + 2 ** 28)
    picked = jnp.argsort(scores, axis=1)[:, :NB - 1]
    others = jnp.take_along_axis(targets, picked, axis=1)
    return jnp.concatenate([leaf_ids[:, None], others], axis=1).astype(jnp.int32)


def draw_far_lists(key, part):
    key = jax.random.fold_in(key, 53)
    devices = LEAVES // LEAF_DEV
    slot_total = devices * CAP
    requests = LEAF_DEV * FAR
    key_owner, key_slot, key_offset, key_order = jax.random.split(key, 4)
    device_ids = jnp.arange(devices, dtype=jnp.int32)
    slot_owner = jnp.repeat(device_ids, CAP)
    slot_rank = jnp.tile(jnp.arange(CAP, dtype=jnp.int32), devices)
    slot_ids = jnp.arange(slot_total, dtype=jnp.int32)

    def one_device(which, owner_key, slot_key, offset_key, order_key):
        allowed = jnp.abs(device_ids - which) > 1
        owner_score = jax.random.randint(owner_key, (devices,), 0, 2 ** 16) * devices + device_ids
        owner_score = jnp.where(allowed, owner_score, owner_score + 2 ** 28)
        forced = jnp.argmin(owner_score)
        slot_score = jax.random.randint(slot_key, (slot_total,), 0, 2 ** 16) * slot_total + slot_ids
        slot_score = jnp.where(slot_owner == forced, slot_ids - slot_total, slot_score)
        slot_score = jnp.where(allowed[slot_owner], slot_score, slot_score + 2 ** 29)
        chosen = jnp.argsort(slot_score)[:requests]
        offsets = jax.random.randint(offset_key, (devices,), 0, LEAF_DEV)
        owner_of = slot_owner[chosen]
        leaves = owner_of * LEAF_DEV + (offsets[owner_of] + slot_rank[chosen]) % LEAF_DEV
        mixing = jnp.argsort(jax.random.randint(order_key, (requests,), 0, 2 ** 20) * requests + jnp.arange(requests))
        return leaves[mixing].reshape(LEAF_DEV, FAR)
    result = jax.vmap(one_device)(device_ids, jax.random.split(key_owner, devices), jax.random.split(key_slot, devices), jax.random.split(key_offset, devices), jax.random.split(key_order, devices))
    return result.reshape(LEAVES, FAR).astype(jnp.int32)


def levels(rng, dims, cuts, least, top_value):
    factor_of = 1.0
    for axis_at, blocks in cuts:
        steps = jax.random.uniform(jax.random.fold_in(jax.random.fold_in(rng, 6), axis_at), (blocks,), jnp.float32, least / len(cuts), top_value / len(cuts))
        factor_of = factor_of * jnp.repeat(jnp.exp(steps), dims[axis_at] // blocks).reshape((-1,) + (1,) * (len(dims) - 1 - axis_at))
    return factor_of


def normal_values(rng, dims, deviation, bound, pieces=(), kind=jnp.bfloat16):
    gain = levels(rng, dims, pieces, -0.22, 0.18) if pieces else 1.0
    values = jax.random.normal(rng, dims, jnp.float32) * deviation * gain
    return jnp.minimum(jnp.maximum(values, -bound), bound).astype(kind)


def setup_inputs(seed: int = 0, part: int = 0) -> dict:
    arg_keys = jax.random.split(jax.random.key(seed), 7)
    part_splits = jax.random.split(jax.random.fold_in(arg_keys[6], part), 7)
    points = draw_points(jax.random.fold_in(jax.random.fold_in(arg_keys[6], part), 71), part)
    weights = normal_values(part_splits[1], (RHS, POINTS), 1.0, 6.0, ((1, 16),))
    interpolation = normal_values(part_splits[2], (LEAVES, LEAF, RANK), LEAF ** -0.5, 0.25, ((0, 16),))
    skeleton = draw_skeleton(jax.random.fold_in(jax.random.fold_in(arg_keys[6], part), 71), part)
    near_lists = draw_near_lists(jax.random.fold_in(jax.random.fold_in(arg_keys[6], part), 71), part)
    far_lists = draw_far_lists(jax.random.fold_in(jax.random.fold_in(arg_keys[6], part), 71), part)
    return dict(points=points, weights=weights, interpolation=interpolation, skeleton=skeleton, near_lists=near_lists, far_lists=far_lists)


amplitude = 0.03
length_sq = 4.0


def kernel_tiles(source, target):
    source_wide = source.astype(jnp.float32)
    target_wide = target.astype(jnp.float32)
    distance = jnp.zeros((source.shape[1], target.shape[1]), jnp.float32)
    for coordinate in range(source.shape[0]):
        offset = source_wide[coordinate][:, None] - target_wide[coordinate][None, :]
        distance = distance + offset * offset
    kernel = amplitude * jnp.exp(distance * (-0.5 / length_sq))
    slope = kernel * distance / length_sq
    return jnp.concatenate([kernel.astype(jnp.bfloat16), slope.astype(jnp.bfloat16)], axis=1)


def leaf_product(target, near_blocks, far_payload, coord_count):
    near_flat = near_blocks.reshape(near_blocks.shape[0], -1)
    tiles = kernel_tiles(near_flat[:coord_count], target)
    near_part = jnp.dot(near_flat[coord_count:], tiles, preferred_element_type=jnp.float32)
    far_flat = far_payload.transpose(1, 0, 2).reshape(far_payload.shape[1], -1)
    far_tiles = kernel_tiles(far_flat[:coord_count], target)
    far_part = jnp.dot(far_flat[coord_count:], far_tiles, preferred_element_type=jnp.float32)
    return near_part + far_part


def skeleton_payload(points, weights, interpolation, skeleton):
    leaves = interpolation.shape[0]
    coord_count = points.shape[0]
    coords = points.reshape(coord_count, leaves, -1).transpose(1, 0, 2)
    indices = jnp.broadcast_to(skeleton[:, None, :], (leaves, coord_count, skeleton.shape[1]))
    chosen = jnp.take_along_axis(coords, indices, axis=2)
    per_leaf = weights.reshape(weights.shape[0], leaves, -1).transpose(1, 0, 2)
    projected = jnp.einsum("bhl,blr->bhr", per_leaf.astype(jnp.float32), interpolation.astype(jnp.float32))
    return jnp.concatenate([chosen, projected.astype(jnp.bfloat16)], axis=1)


def reference(points, weights, interpolation, skeleton, near_lists, far_lists):
    leaves = interpolation.shape[0]
    leaf_size = interpolation.shape[1]
    coord_count = points.shape[0]
    payload = skeleton_payload(points, weights, interpolation, skeleton)
    stacked = jnp.concatenate([points, weights], axis=0).reshape(-1, leaves, leaf_size)

    def one_leaf(inputs):
        leaf_id, near_ids, far_ids = inputs
        target = lax.dynamic_index_in_dim(stacked[:coord_count], leaf_id, 1, keepdims=False)
        near_blocks = jnp.take(stacked, near_ids, axis=1)
        far_payload = jnp.take(payload, far_ids, axis=0)
        return leaf_product(target, near_blocks, far_payload, coord_count)

    results = lax.map(one_leaf, (jnp.arange(leaves, dtype=jnp.int32), near_lists, far_lists))
    kernel_product = results[:, :, :leaf_size].transpose(1, 0, 2).reshape(weights.shape[0], -1)
    derivative_product = results[:, :, leaf_size:].transpose(1, 0, 2).reshape(weights.shape[0], -1)
    return (kernel_product, derivative_product)
```

```python
import functools

import jax
import jax.numpy as jnp
from jax import lax
from jax.experimental import pallas as pl
from jax.experimental.pallas import tpu as pltpu
from jax.sharding import PartitionSpec as P

amplitude = 0.03
length_sq = 4.0
log2_e = 1.4426950408889634
rate = -0.5 / length_sq * log2_e
MIB = 1024 * 1024


def pieces(x):
    high = x.astype(jnp.bfloat16).astype(jnp.float32)
    rest = x - high
    middle = rest.astype(jnp.bfloat16).astype(jnp.float32)
    low = (rest - middle).astype(jnp.bfloat16).astype(jnp.float32)
    return high, middle, low


def norm_rows(coords, first):
    norms = pieces(rate * jnp.sum(coords * coords, axis=0, keepdims=True))
    row = lax.broadcasted_iota(jnp.int32, coords.shape, 0)
    out = jnp.where(row < 6, 1.0, 0.0)
    for at, piece in enumerate(norms):
        out = jnp.where(row == first + at, piece, out)
    return out


def source_factor(coords):
    high, middle, low = pieces(coords * (-2.0 * rate))
    return jnp.concatenate([high, middle, low, norm_rows(coords, 0)], axis=0).astype(jnp.bfloat16)


def target_factor(coords):
    stacked = jnp.concatenate([coords, coords, coords, norm_rows(coords, 3)], axis=0)
    return stacked.T.astype(jnp.bfloat16)


def accumulate(targets, factor, weights):
    exponent = jnp.dot(targets, factor, preferred_element_type=jnp.float32)
    kernel = jnp.exp2(exponent)
    slope = kernel * exponent
    over_sources = (((1,), (1,)), ((), ()))
    return (
        lax.dot_general(kernel.astype(jnp.bfloat16), weights, over_sources, preferred_element_type=jnp.float32),
        lax.dot_general(slope.astype(jnp.bfloat16), weights, over_sources, preferred_element_type=jnp.float32),
    )


def payload_kernel(points_ref, weights_ref, interpolation_ref, skeleton_ref, out_ref):
    leaves, leaf_size, rank = interpolation_ref.shape
    half = rank // 2
    rhs = weights_ref.shape[0]
    dim = points_ref.shape[0]
    for leaf in range(leaves):
        columns = pl.ds(leaf * leaf_size, leaf_size)
        projected = jnp.dot(
            weights_ref[:, columns], interpolation_ref[leaf], preferred_element_type=jnp.float32
        ).astype(jnp.bfloat16)
        position = lax.broadcasted_iota(jnp.int32, (leaf_size, rank), 0)
        selector = jnp.where(position == skeleton_ref[leaf : leaf + 1, :], 1.0, 0.0).astype(jnp.bfloat16)
        chosen = jnp.dot(points_ref[:, columns], selector, preferred_element_type=jnp.float32)
        out_ref[leaf, 0:rhs] = projected[:, :half]
        out_ref[leaf, rhs : 2 * rhs] = projected[:, half:]
        both = jnp.concatenate([chosen[:, :half], chosen[:, half:]], axis=0)
        out_ref[leaf, 2 * rhs : 2 * rhs + 2 * dim] = both.astype(jnp.bfloat16)


def near_kernel(
    lists_ref, points_prev, points_own, points_next, weights_prev, weights_own, weights_next,
    kernel_ref, slope_ref, factor_ref, weight_ref, target_ref, kernel_acc, slope_acc,
):
    leaves, near = lists_ref.shape
    leaf_size = factor_ref.shape[2]
    for side, (points, weights) in enumerate(
        ((points_prev, weights_prev), (points_own, weights_own), (points_next, weights_next))
    ):
        for leaf in range(leaves):
            columns = pl.ds(leaf * leaf_size, leaf_size)
            coords = points[:, columns].astype(jnp.float32)
            factor_ref[side * leaves + leaf] = source_factor(coords)
            weight_ref[side * leaves + leaf] = weights[:, columns]
            if side == 1:
                target_ref[leaf] = target_factor(coords)

    @pl.loop(0, leaves)
    def _(leaf):
        kernel_acc[...] = jnp.zeros_like(kernel_acc)
        slope_acc[...] = jnp.zeros_like(slope_acc)

        @pl.loop(0, near)
        def _(slot):
            source = lists_ref[leaf, slot]
            kernel, slope = accumulate(target_ref[leaf], factor_ref[source], weight_ref[source])
            kernel_acc[...] += kernel
            slope_acc[...] += slope

        columns = pl.ds(pl.multiple_of(leaf * leaf_size, leaf_size), leaf_size)
        kernel_ref[:, columns] = kernel_acc[...].T
        slope_ref[:, columns] = slope_acc[...].T


def far_kernel(
    lists_ref, points_ref, near_kernel_ref, near_slope_ref, everything_ref,
    kernel_ref, slope_ref, block_ref, kernel_acc, slope_acc, semaphore,
):
    leaves, far = lists_ref.shape
    leaf_size = points_ref.shape[1] // leaves
    rows = block_ref.shape[2]
    dim = points_ref.shape[0]
    rhs = kernel_ref.shape[0]

    def fetch(leaf, slot):
        return pltpu.make_async_copy(
            everything_ref.at[lists_ref[leaf, slot]], block_ref.at[leaf, slot], semaphore.at[leaf, slot]
        )

    @pl.loop(0, leaves)
    def _(leaf):
        @pl.loop(0, far)
        def _(slot):
            fetch(leaf, slot).start()

    @pl.loop(0, leaves)
    def _(leaf):
        columns = pl.ds(pl.multiple_of(leaf * leaf_size, leaf_size), leaf_size)
        targets = target_factor(points_ref[:, columns].astype(jnp.float32))
        kernel_acc[...] = jnp.zeros_like(kernel_acc)
        slope_acc[...] = jnp.zeros_like(slope_acc)

        @pl.loop(0, far // 2)
        def _(pair):
            halves = []
            coords = []
            for member in range(2):
                slot = pair * 2 + member
                fetch(leaf, slot).wait()
                for part in range(2):
                    halves.append(block_ref[leaf, slot, part * rhs : (part + 1) * rhs])
                both = block_ref[leaf, slot, 2 * rhs : rows].astype(jnp.float32)
                coords += [both[:dim], both[dim:]]
            factor = source_factor(jnp.concatenate(coords, axis=1))
            kernel, slope = accumulate(targets, factor, jnp.concatenate(halves, axis=1))
            kernel_acc[...] += kernel
            slope_acc[...] += slope

        kernel_ref[:, columns] = amplitude * (near_kernel_ref[:, columns] + kernel_acc[...].T)
        slope_ref[:, columns] = (amplitude / (length_sq * rate)) * (near_slope_ref[:, columns] + slope_acc[...].T)


def local(points, weights, interpolation, skeleton, near_lists, far_lists):
    position = lax.axis_index("leaf")
    count = lax.axis_size("leaf")
    leaves, leaf_size, rank = interpolation.shape
    dim, rhs = points.shape[0], weights.shape[0]
    far, near = far_lists.shape[1], near_lists.shape[1]
    width = points.shape[1]
    vmem = pl.BlockSpec(memory_space=pltpu.VMEM)
    smem = pl.BlockSpec(memory_space=pltpu.SMEM)
    up = [(i, i + 1) for i in range(count - 1)]
    down = [(i + 1, i) for i in range(count - 1)]
    points_prev, weights_prev = lax.ppermute(points, "leaf", up), lax.ppermute(weights, "leaf", up)
    points_next, weights_next = lax.ppermute(points, "leaf", down), lax.ppermute(weights, "leaf", down)

    rows = 2 * (rhs + dim)
    payload = pl.pallas_call(
        payload_kernel,
        out_shape=jax.ShapeDtypeStruct((leaves, rows, rank // 2), jnp.bfloat16),
        in_specs=[vmem] * 4,
        out_specs=vmem,
        compiler_params=pltpu.CompilerParams(vmem_limit_bytes=32 * MIB),
        cost_estimate=pl.CostEstimate(
            flops=2 * leaves * (rhs + dim) * leaf_size * rank, bytes_accessed=interpolation.size * 2, transcendentals=0
        ),
    )(points, weights, interpolation, skeleton)
    everything = lax.all_gather(payload, "leaf", axis=0, tiled=True)

    def cost(sources):
        pairs = leaves * leaf_size * sources
        return pl.CostEstimate(
            flops=pairs * 2 * (256 + 512), bytes_accessed=6 * rhs * width * 2, transcendentals=pairs
        )

    partial = jax.ShapeDtypeStruct((rhs, width), jnp.float32)
    accumulator = pltpu.VMEM((leaf_size, rhs), jnp.float32)
    local_near = near_lists - (position - 1) * leaves
    near_kernel_part, near_slope_part = pl.pallas_call(
        near_kernel,
        out_shape=(partial, partial),
        in_specs=[smem] + [vmem] * 6,
        out_specs=(vmem, vmem),
        scratch_shapes=[
            pltpu.VMEM((3 * leaves, 4 * dim, leaf_size), jnp.bfloat16),
            pltpu.VMEM((3 * leaves, rhs, leaf_size), jnp.bfloat16),
            pltpu.VMEM((leaves, leaf_size, 4 * dim), jnp.bfloat16),
            accumulator,
            accumulator,
        ],
        compiler_params=pltpu.CompilerParams(vmem_limit_bytes=48 * MIB),
        cost_estimate=cost(near * leaf_size),
    )(local_near, points_prev, points, points_next, weights_prev, weights, weights_next)

    return pl.pallas_call(
        far_kernel,
        out_shape=(partial, partial),
        in_specs=[smem, vmem, vmem, vmem, pl.BlockSpec(memory_space=pl.ANY)],
        out_specs=(vmem, vmem),
        scratch_shapes=[
            pltpu.VMEM((leaves, far, rows, rank // 2), jnp.bfloat16),
            accumulator,
            accumulator,
            pltpu.SemaphoreType.DMA((leaves, far)),
        ],
        compiler_params=pltpu.CompilerParams(vmem_limit_bytes=48 * MIB),
        cost_estimate=cost(far * rank),
    )(far_lists, points, near_kernel_part, near_slope_part, everything)


def solution(mesh):
    placed = (
        P(None, ("groups", "leaf")),
        P(None, ("groups", "leaf")),
        P(("groups", "leaf"), None, None),
        P(("groups", "leaf"), None),
        P(("groups", "leaf"), None),
        P(("groups", "leaf"), None),
    )
    return jax.shard_map(
        local,
        mesh=mesh,
        in_specs=placed,
        out_specs=(P(None, ("groups", "leaf")), P(None, ("groups", "leaf"))),
        check_vma=False,
    )
```

```python
import functools

import jax
import jax.numpy as jnp
from jax import lax
from jax.experimental import pallas as pl
from jax.experimental.pallas import tpu as pltpu
from jax.sharding import PartitionSpec as P

amplitude = 0.03
length_sq = 4.0
log2_e = 1.4426950408889634
rate = -0.5 / length_sq * log2_e
MIB = 1024 * 1024


def pieces(x):
    high = x.astype(jnp.bfloat16).astype(jnp.float32)
    rest = x - high
    middle = rest.astype(jnp.bfloat16).astype(jnp.float32)
    low = (rest - middle).astype(jnp.bfloat16).astype(jnp.float32)
    return high, middle, low


def norm_rows(coords, first):
    norms = pieces(rate * jnp.sum(coords * coords, axis=0, keepdims=True))
    row = lax.broadcasted_iota(jnp.int32, coords.shape, 0)
    out = jnp.where(row < 6, 1.0, 0.0)
    for at, piece in enumerate(norms):
        out = jnp.where(row == first + at, piece, out)
    return out


def source_factor(coords):
    high, middle, low = pieces(coords * (-2.0 * rate))
    return jnp.concatenate([high, middle, low, norm_rows(coords, 0)], axis=0).astype(jnp.bfloat16)


def target_factor(coords):
    stacked = jnp.concatenate([coords, coords, coords, norm_rows(coords, 3)], axis=0)
    return stacked.T.astype(jnp.bfloat16)


def accumulate(targets, factor, weights):
    exponent = jnp.dot(targets, factor, preferred_element_type=jnp.float32)
    kernel = jnp.exp2(exponent)
    slope = kernel * exponent
    over_sources = (((1,), (1,)), ((), ()))
    return (
        lax.dot_general(kernel.astype(jnp.bfloat16), weights, over_sources, preferred_element_type=jnp.float32),
        lax.dot_general(slope.astype(jnp.bfloat16), weights, over_sources, preferred_element_type=jnp.float32),
    )


def skeleton_block(points_ref, weights_ref, interpolation_ref, skeleton_ref, out_ref):
    leaves, leaf_size, rank = interpolation_ref.shape
    half = rank // 2
    rhs = weights_ref.shape[0]
    dim = points_ref.shape[0]
    for leaf in range(leaves):
        columns = pl.ds(leaf * leaf_size, leaf_size)
        projected = jnp.dot(
            weights_ref[:, columns], interpolation_ref[leaf], preferred_element_type=jnp.float32
        ).astype(jnp.bfloat16)
        position = lax.broadcasted_iota(jnp.int32, (leaf_size, rank), 0)
        selector = jnp.where(position == skeleton_ref[leaf : leaf + 1, :], 1.0, 0.0).astype(jnp.bfloat16)
        chosen = jnp.dot(points_ref[:, columns], selector, preferred_element_type=jnp.float32)
        out_ref[leaf, 0:rhs] = projected[:, :half]
        out_ref[leaf, rhs : 2 * rhs] = projected[:, half:]
        both = jnp.concatenate([chosen[:, :half], chosen[:, half:]], axis=0)
        out_ref[leaf, 2 * rhs : 2 * rhs + 2 * dim] = both.astype(jnp.bfloat16)


def near_kernel(
    count, lists_ref, points_ref, weights_ref, interpolation_ref, skeleton_ref,
    kernel_ref, slope_ref, all_ref,
    factor_ref, weight_ref, target_ref, kernel_acc, slope_acc,
    payload_ref, packed_ref, halo_points, halo_weights,
    own_sem, halo_send, halo_recv, up_send, up_recv, down_send, down_recv,
    across_send, across_recv, core_send, core_recv,
):
    leaves, near = lists_ref.shape
    leaf_size = factor_ref.shape[2]
    dim = points_ref.shape[0]
    middle = packed_ref.shape[1]
    me = lax.axis_index("leaf")
    length = count // 4
    place, lane = me // 4, lax.rem(me, 4)
    row, core = lane // 2, lax.rem(lane, 2)
    across = place * 4 + (1 - row) * 2 + core
    sibling = place * 4 + row * 2 + (1 - core)
    has_prev, has_next = me > 0, me < count - 1
    has_low, has_high = place > 0, place < length - 1

    def remote(source, target, send, recv, device):
        return pltpu.make_async_remote_copy(
            src_ref=source, dst_ref=target, send_sem=send, recv_sem=recv,
            device_id={"leaf": device}, device_id_type=pl.DeviceIdType.MESH,
        )

    barrier = pltpu.get_barrier_semaphore()

    def greet(device):
        pl.semaphore_signal(barrier, inc=1, device_id={"leaf": device}, device_id_type=pl.DeviceIdType.MESH)

    greet(across)
    greet(sibling)
    others = (
        (jnp.logical_and(has_prev, core == 0), me - 1), (jnp.logical_and(has_next, core == 1), me + 1),
        (has_low, me - 4), (has_high, me + 4),
    )
    peers = 2
    for present, device in others:
        peers = peers + present.astype(jnp.int32)

        @pl.when(present)
        def _(device=device):
            greet(device)

    packed_ref[...] = jnp.concatenate(
        [points_ref[:, :middle].astype(jnp.float32), points_ref[:, middle:].astype(jnp.float32)], axis=0
    ).astype(jnp.bfloat16)
    pl.semaphore_wait(barrier, peers)

    def halo(side, device):
        return (
            remote(packed_ref, halo_points.at[side], halo_send.at[side, 0], halo_recv.at[side, 0], device),
            remote(weights_ref, halo_weights.at[side], halo_send.at[side, 1], halo_recv.at[side, 1], device),
        )

    to_next, to_prev = halo(0, me + 1), halo(1, me - 1)
    for present, copies in ((has_next, to_next), (has_prev, to_prev)):

        @pl.when(present)
        def _(copies=copies):
            for copy in copies:
                copy.start()

    for present, side in ((has_prev, 0), (has_next, 1)):

        @pl.when(jnp.logical_not(present))
        def _(side=side):
            halo_points[side] = jnp.zeros_like(halo_points[side])
            halo_weights[side] = jnp.zeros_like(halo_weights[side])

    skeleton_block(points_ref, weights_ref, interpolation_ref, skeleton_ref, payload_ref)

    def slot(place_of, lane_of):
        return all_ref.at[pl.ds((place_of * 4 + lane_of) * leaves, leaves)]

    def up(step):
        source = payload_ref if step == 0 else slot(place - step, lane)
        return remote(source, slot(place - step, lane), up_send.at[step], up_recv.at[step + 1], me + 4)

    def down(step):
        source = payload_ref if step == 0 else slot(place + step, lane)
        return remote(source, slot(place + step, lane), down_send.at[step], down_recv.at[step + 1], me - 4)

    def over(place_of, source=None):
        block = slot(place_of, lane)
        return remote(
            block if source is None else source, block, across_send.at[place_of], across_recv.at[place_of], across
        )

    def share(place_of, row_of, source=None):
        block = slot(place_of, row_of * 2 + core)
        return remote(
            block if source is None else source, block,
            core_send.at[place_of, row_of], core_recv.at[place_of, row_of], sibling,
        )

    own = pltpu.make_async_copy(payload_ref, slot(place, lane), own_sem)
    own.start()
    over(place, payload_ref).start()
    share(place, row, payload_ref).start()
    for present, first in ((has_high, up(0)), (has_low, down(0))):

        @pl.when(present)
        def _(first=first):
            first.start()

    def arrived_along(step):
        @pl.when(place - step >= 0)
        def _():
            remote(payload_ref, slot(place - step, lane), up_send.at[0], up_recv.at[step], me + 4).wait_recv()

            @pl.when(has_high)
            def _():
                up(step).start()

            over(place - step).start()
            share(place - step, row).start()

        @pl.when(place + step < length)
        def _():
            remote(payload_ref, slot(place + step, lane), down_send.at[0], down_recv.at[step], me - 4).wait_recv()

            @pl.when(has_low)
            def _():
                down(step).start()

            over(place + step).start()
            share(place + step, row).start()

    def arrived_across(step):
        def one(place_of):
            remote(
                payload_ref, slot(place_of, (1 - row) * 2 + core), across_send.at[place_of],
                across_recv.at[place_of], across,
            ).wait_recv()
            share(place_of, 1 - row).start()

        if step == 0:
            one(place)
            return

        @pl.when(place - step >= 0)
        def _():
            one(place - step)

        @pl.when(place + step < length)
        def _():
            one(place + step)

    @pl.loop(0, leaves)
    def _(leaf):
        columns = pl.ds(pl.multiple_of(leaf * leaf_size, leaf_size), leaf_size)
        coords = points_ref[:, columns].astype(jnp.float32)
        factor_ref[leaves + leaf] = source_factor(coords)
        weight_ref[leaves + leaf] = weights_ref[:, columns]
        target_ref[leaf] = target_factor(coords)
        kernel, slope = accumulate(target_ref[leaf], factor_ref[leaves + leaf], weight_ref[leaves + leaf])
        kernel_acc[leaf] = kernel
        slope_acc[leaf] = slope

    for present, copies in ((has_prev, halo(0, me + 1)), (has_next, halo(1, me - 1))):

        @pl.when(present)
        def _(copies=copies):
            for copy in copies:
                copy.wait_recv()

    for side in range(2):
        for leaf in range(leaves):
            begin = leaf * leaf_size
            part, begin_in = begin // middle, begin % middle
            both = halo_points[side, :, begin_in : begin_in + leaf_size].astype(jnp.float32)
            coords = both[part * dim : (part + 1) * dim]
            factor_ref[2 * leaves * side + leaf] = source_factor(coords)
            weight_ref[2 * leaves * side + leaf] = halo_weights[side, :, begin : begin + leaf_size]

    def run_leaves(first, last):
        @pl.loop(first, last)
        def _(leaf):
            @pl.loop(1, near)
            def _(entry):
                source = lists_ref[leaf, entry]
                kernel, slope = accumulate(target_ref[leaf], factor_ref[source], weight_ref[source])
                kernel_acc[leaf] += kernel
                slope_acc[leaf] += slope

            columns = pl.ds(pl.multiple_of(leaf * leaf_size, leaf_size), leaf_size)
            kernel_ref[:, columns] = kernel_acc[leaf].T
            slope_ref[:, columns] = slope_acc[leaf].T

    done = 0
    for step in range(1, length):
        upto = min(leaves - 1, max(done, step * (leaves - 1) // length + 1))
        if upto > done:
            run_leaves(done, upto)
            done = upto
        arrived_along(step)
        arrived_across(step - 1)
    run_leaves(done, leaves)
    arrived_across(length - 1)

    own.wait()
    for present, copies in ((has_next, to_next), (has_prev, to_prev)):

        @pl.when(present)
        def _(copies=copies):
            for copy in copies:
                copy.wait_send()

    for step in range(length):
        for present, there, copy in (
            (has_high, place - step >= 0, up(step)), (has_low, place + step < length, down(step)),
        ):

            @pl.when(jnp.logical_and(present, there))
            def _(copy=copy):
                copy.wait_send()

    for place_of in range(length):
        over(place_of).wait_send()
        for row_of in range(2):
            share(place_of, row_of).wait_send()
            remote(
                payload_ref, slot(place_of, row_of * 2 + 1 - core), core_send.at[place_of, row_of],
                core_recv.at[place_of, row_of], sibling,
            ).wait_recv()


def far_kernel(
    lists_ref, points_ref, near_kernel_ref, near_slope_ref, everything_ref,
    kernel_ref, slope_ref, block_ref, kernel_acc, slope_acc, semaphore,
):
    leaves, far = lists_ref.shape
    leaf_size = points_ref.shape[1] // leaves
    rows = block_ref.shape[2]
    dim = points_ref.shape[0]
    rhs = kernel_ref.shape[0]

    def fetch(leaf, slot):
        return pltpu.make_async_copy(
            everything_ref.at[lists_ref[leaf, slot]], block_ref.at[leaf, slot], semaphore.at[leaf, slot]
        )

    @pl.loop(0, leaves)
    def _(leaf):
        @pl.loop(0, far)
        def _(slot):
            fetch(leaf, slot).start()

    @pl.loop(0, leaves)
    def _(leaf):
        columns = pl.ds(pl.multiple_of(leaf * leaf_size, leaf_size), leaf_size)
        targets = target_factor(points_ref[:, columns].astype(jnp.float32))
        kernel_acc[...] = jnp.zeros_like(kernel_acc)
        slope_acc[...] = jnp.zeros_like(slope_acc)

        @pl.loop(0, far // 2)
        def _(pair):
            halves = []
            coords = []
            for member in range(2):
                slot = pair * 2 + member
                fetch(leaf, slot).wait()
                for part in range(2):
                    halves.append(block_ref[leaf, slot, part * rhs : (part + 1) * rhs])
                both = block_ref[leaf, slot, 2 * rhs : rows].astype(jnp.float32)
                coords += [both[:dim], both[dim:]]
            factor = source_factor(jnp.concatenate(coords, axis=1))
            kernel, slope = accumulate(targets, factor, jnp.concatenate(halves, axis=1))
            kernel_acc[...] += kernel
            slope_acc[...] += slope

        kernel_ref[:, columns] = amplitude * (near_kernel_ref[:, columns] + kernel_acc[...].T)
        slope_ref[:, columns] = (amplitude / (length_sq * rate)) * (near_slope_ref[:, columns] + slope_acc[...].T)


def local(points, weights, interpolation, skeleton, near_lists, far_lists):
    position = lax.axis_index("leaf")
    count = lax.axis_size("leaf")
    leaves, leaf_size, rank = interpolation.shape
    dim, rhs = points.shape[0], weights.shape[0]
    far, near = far_lists.shape[1], near_lists.shape[1]
    width = points.shape[1]
    vmem = pl.BlockSpec(memory_space=pltpu.VMEM)
    smem = pl.BlockSpec(memory_space=pltpu.SMEM)
    rows = 2 * (rhs + dim)

    def cost(sources):
        pairs = leaves * leaf_size * sources
        return pl.CostEstimate(
            flops=pairs * 2 * (256 + 512), bytes_accessed=6 * rhs * width * 2, transcendentals=pairs
        )

    partial = jax.ShapeDtypeStruct((rhs, width), jnp.float32)
    accumulator = pltpu.VMEM((leaf_size, rhs), jnp.float32)
    local_near = near_lists - (position - 1) * leaves
    dma = pltpu.SemaphoreType.DMA
    length = count // 4
    near_kernel_part, near_slope_part, everything = pl.pallas_call(
        functools.partial(near_kernel, count),
        out_shape=(partial, partial, jax.ShapeDtypeStruct((count * leaves, rows, rank // 2), jnp.bfloat16)),
        in_specs=[smem] + [vmem] * 4,
        out_specs=(vmem, vmem, pl.BlockSpec(memory_space=pl.ANY)),
        scratch_shapes=[
            pltpu.VMEM((3 * leaves, 4 * dim, leaf_size), jnp.bfloat16),
            pltpu.VMEM((3 * leaves, rhs, leaf_size), jnp.bfloat16),
            pltpu.VMEM((leaves, leaf_size, 4 * dim), jnp.bfloat16),
            pltpu.VMEM((leaves, leaf_size, rhs), jnp.float32),
            pltpu.VMEM((leaves, leaf_size, rhs), jnp.float32),
            pltpu.VMEM((leaves, rows, rank // 2), jnp.bfloat16),
            pltpu.VMEM((2 * dim, width // 2), jnp.bfloat16),
            pltpu.VMEM((2, 2 * dim, width // 2), jnp.bfloat16),
            pltpu.VMEM((2, rhs, width), jnp.bfloat16),
            dma(()),
            dma((2, 2)), dma((2, 2)),
            dma((length + 1,)), dma((length + 1,)), dma((length + 1,)), dma((length + 1,)),
            dma((length,)), dma((length,)),
            dma((length, 2)), dma((length, 2)),
        ],
        compiler_params=pltpu.CompilerParams(
            collective_id=0, has_side_effects=True, vmem_limit_bytes=48 * MIB
        ),
        cost_estimate=cost(near * leaf_size),
    )(local_near, points, weights, interpolation, skeleton)

    return pl.pallas_call(
        far_kernel,
        out_shape=(partial, partial),
        in_specs=[smem, vmem, vmem, vmem, pl.BlockSpec(memory_space=pl.ANY)],
        out_specs=(vmem, vmem),
        scratch_shapes=[
            pltpu.VMEM((leaves, far, rows, rank // 2), jnp.bfloat16),
            accumulator,
            accumulator,
            pltpu.SemaphoreType.DMA((leaves, far)),
        ],
        compiler_params=pltpu.CompilerParams(vmem_limit_bytes=48 * MIB),
        cost_estimate=cost(far * rank),
    )(far_lists, points, near_kernel_part, near_slope_part, everything)


def solution(mesh):
    placed = (
        P(None, ("groups", "leaf")),
        P(None, ("groups", "leaf")),
        P(("groups", "leaf"), None, None),
        P(("groups", "leaf"), None),
        P(("groups", "leaf"), None),
        P(("groups", "leaf"), None),
    )
    return jax.shard_map(
        local,
        mesh=mesh,
        in_specs=placed,
        out_specs=(P(None, ("groups", "leaf")), P(None, ("groups", "leaf"))),
        check_vma=False,
    )
```

```python
import functools

import jax
import jax.numpy as jnp
from jax import lax
from jax.experimental import pallas as pl
from jax.experimental.pallas import tpu as pltpu
from jax.sharding import PartitionSpec as P

amplitude = 0.03
length_sq = 4.0
log2_e = 1.4426950408889634
rate = -0.5 / length_sq * log2_e
MIB = 1024 * 1024


def pieces(x):
    high = x.astype(jnp.bfloat16).astype(jnp.float32)
    rest = x - high
    middle = rest.astype(jnp.bfloat16).astype(jnp.float32)
    low = (rest - middle).astype(jnp.bfloat16).astype(jnp.float32)
    return high, middle, low


def norm_rows(coords, first):
    norms = pieces(rate * jnp.sum(coords * coords, axis=0, keepdims=True))
    row = lax.broadcasted_iota(jnp.int32, coords.shape, 0)
    out = jnp.where(row < 6, 1.0, 0.0)
    for at, piece in enumerate(norms):
        out = jnp.where(row == first + at, piece, out)
    return out


def source_factor(coords):
    high, middle, low = pieces(coords * (-2.0 * rate))
    return jnp.concatenate([high, middle, low, norm_rows(coords, 0)], axis=0).T.astype(jnp.bfloat16)


def target_factor(coords):
    return jnp.concatenate([coords, coords, coords, norm_rows(coords, 3)], axis=0).astype(jnp.bfloat16)


def products(factors, weights, targets):
    kernels, slopes = [], []
    for factor in factors:
        exponent = jnp.dot(factor, targets, preferred_element_type=jnp.float32)
        kernel = jnp.exp2(exponent)
        kernels.append(kernel.astype(jnp.bfloat16))
        slopes.append((kernel * exponent).astype(jnp.bfloat16))
    return (
        jnp.dot(weights, jnp.concatenate(kernels, axis=0), preferred_element_type=jnp.float32),
        jnp.dot(weights, jnp.concatenate(slopes, axis=0), preferred_element_type=jnp.float32),
    )


def skeleton_block(points_ref, weights_ref, interpolation_ref, skeleton_ref, out_ref):
    leaves, leaf_size, rank = interpolation_ref.shape
    half = rank // 2
    rhs = weights_ref.shape[0]
    dim = points_ref.shape[0]
    for leaf in range(leaves):
        columns = pl.ds(leaf * leaf_size, leaf_size)
        projected = jnp.dot(
            weights_ref[:, columns], interpolation_ref[leaf], preferred_element_type=jnp.float32
        ).astype(jnp.bfloat16)
        position = lax.broadcasted_iota(jnp.int32, (leaf_size, rank), 0)
        selector = jnp.where(position == skeleton_ref[leaf : leaf + 1, :], 1.0, 0.0).astype(jnp.bfloat16)
        chosen = jnp.dot(points_ref[:, columns], selector, preferred_element_type=jnp.float32)
        out_ref[leaf, 0:rhs] = projected[:, :half]
        out_ref[leaf, rhs : 2 * rhs] = projected[:, half:]
        both = jnp.concatenate([chosen[:, :half], chosen[:, half:]], axis=0)
        out_ref[leaf, 2 * rhs : 2 * rhs + 2 * dim] = both.astype(jnp.bfloat16)


def near_kernel(
    count, lists_ref, points_ref, weights_ref, interpolation_ref, skeleton_ref,
    kernel_ref, slope_ref, all_ref,
    factor_ref, weight_ref, target_ref,
    payload_ref, packed_ref, halo_points, halo_weights, interpolation_vmem,
    own_sem, load_sem, halo_send, halo_recv, up_send, up_recv, down_send, down_recv,
    across_send, across_recv, core_send, core_recv,
):
    leaves, near = lists_ref.shape
    leaf_size = factor_ref.shape[1]
    tile = leaf_size // 2
    first_leaf = (lax.axis_index("leaf") - 1) * leaves
    dim = points_ref.shape[0]
    middle = packed_ref.shape[1]
    me = lax.axis_index("leaf")
    length = count // 4
    place, lane = me // 4, lax.rem(me, 4)
    row, core = lane // 2, lax.rem(lane, 2)
    across = place * 4 + (1 - row) * 2 + core
    sibling = place * 4 + row * 2 + (1 - core)
    has_prev, has_next = me > 0, me < count - 1
    has_low, has_high = place > 0, place < length - 1

    def remote(source, target, send, recv, device):
        return pltpu.make_async_remote_copy(
            src_ref=source, dst_ref=target, send_sem=send, recv_sem=recv,
            device_id={"leaf": device}, device_id_type=pl.DeviceIdType.MESH,
        )

    load = pltpu.make_async_copy(interpolation_ref, interpolation_vmem, load_sem)
    load.start()
    barrier = pltpu.get_barrier_semaphore()

    def greet(device):
        pl.semaphore_signal(barrier, inc=1, device_id={"leaf": device}, device_id_type=pl.DeviceIdType.MESH)

    greet(across)
    greet(sibling)
    others = (
        (jnp.logical_and(has_prev, core == 0), me - 1), (jnp.logical_and(has_next, core == 1), me + 1),
        (has_low, me - 4), (has_high, me + 4),
    )
    peers = 2
    for present, device in others:
        peers = peers + present.astype(jnp.int32)

        @pl.when(present)
        def _(device=device):
            greet(device)

    packed_ref[...] = jnp.concatenate(
        [points_ref[:, :middle].astype(jnp.float32), points_ref[:, middle:].astype(jnp.float32)], axis=0
    ).astype(jnp.bfloat16)
    pl.semaphore_wait(barrier, peers)

    def halo(side, device):
        return (
            remote(packed_ref, halo_points.at[side], halo_send.at[side, 0], halo_recv.at[side, 0], device),
            remote(weights_ref, halo_weights.at[side], halo_send.at[side, 1], halo_recv.at[side, 1], device),
        )

    to_next, to_prev = halo(0, me + 1), halo(1, me - 1)
    for present, copies in ((has_next, to_next), (has_prev, to_prev)):

        @pl.when(present)
        def _(copies=copies):
            for copy in copies:
                copy.start()

    for present, side in ((has_prev, 0), (has_next, 1)):

        @pl.when(jnp.logical_not(present))
        def _(side=side):
            halo_points[side] = jnp.zeros_like(halo_points[side])
            halo_weights[side] = jnp.zeros_like(halo_weights[side])

    load.wait()
    skeleton_block(points_ref, weights_ref, interpolation_vmem, skeleton_ref, payload_ref)

    def slot(place_of, lane_of):
        return all_ref.at[pl.ds((place_of * 4 + lane_of) * leaves, leaves)]

    def up(step):
        source = payload_ref if step == 0 else slot(place - step, lane)
        return remote(source, slot(place - step, lane), up_send.at[step], up_recv.at[step + 1], me + 4)

    def down(step):
        source = payload_ref if step == 0 else slot(place + step, lane)
        return remote(source, slot(place + step, lane), down_send.at[step], down_recv.at[step + 1], me - 4)

    def over(place_of, source=None):
        block = slot(place_of, lane)
        return remote(
            block if source is None else source, block, across_send.at[place_of], across_recv.at[place_of], across
        )

    def share(place_of, row_of, source=None):
        block = slot(place_of, row_of * 2 + core)
        return remote(
            block if source is None else source, block,
            core_send.at[place_of, row_of], core_recv.at[place_of, row_of], sibling,
        )

    own = pltpu.make_async_copy(payload_ref, slot(place, lane), own_sem)
    own.start()
    over(place, payload_ref).start()
    share(place, row, payload_ref).start()
    for present, first in ((has_high, up(0)), (has_low, down(0))):

        @pl.when(present)
        def _(first=first):
            first.start()

    def arrived_along(step):
        @pl.when(place - step >= 0)
        def _():
            remote(payload_ref, slot(place - step, lane), up_send.at[0], up_recv.at[step], me + 4).wait_recv()

            @pl.when(has_high)
            def _():
                up(step).start()

            over(place - step).start()
            share(place - step, row).start()

        @pl.when(place + step < length)
        def _():
            remote(payload_ref, slot(place + step, lane), down_send.at[0], down_recv.at[step], me - 4).wait_recv()

            @pl.when(has_low)
            def _():
                down(step).start()

            over(place + step).start()
            share(place + step, row).start()

    def arrived_across(step):
        def one(place_of):
            remote(
                payload_ref, slot(place_of, (1 - row) * 2 + core), across_send.at[place_of],
                across_recv.at[place_of], across,
            ).wait_recv()
            share(place_of, 1 - row).start()

        if step == 0:
            one(place)
            return

        @pl.when(place - step >= 0)
        def _():
            one(place - step)

        @pl.when(place + step < length)
        def _():
            one(place + step)

    @pl.loop(0, leaves)
    def _(leaf):
        columns = pl.ds(pl.multiple_of(leaf * leaf_size, leaf_size), leaf_size)
        coords = points_ref[:, columns].astype(jnp.float32)
        factor_ref[leaves + leaf] = source_factor(coords)
        weight_ref[leaves + leaf] = weights_ref[:, columns]
        target_ref[leaf] = target_factor(coords)
        kernel_ref[:, columns], slope_ref[:, columns] = products(
            [factor_ref[leaves + leaf]], weight_ref[leaves + leaf], target_ref[leaf]
        )

    for present, copies in ((has_prev, halo(0, me + 1)), (has_next, halo(1, me - 1))):

        @pl.when(present)
        def _(copies=copies):
            for copy in copies:
                copy.wait_recv()

    for side in range(2):
        for leaf in range(leaves):
            begin = leaf * leaf_size
            part, begin_in = begin // middle, begin % middle
            both = halo_points[side, :, begin_in : begin_in + leaf_size].astype(jnp.float32)
            coords = both[part * dim : (part + 1) * dim]
            factor_ref[2 * leaves * side + leaf] = source_factor(coords)
            weight_ref[2 * leaves * side + leaf] = halo_weights[side, :, begin : begin + leaf_size]

    def run_leaves(first, last):
        @pl.loop(first, last)
        def _(leaf):
            sources = [
                jnp.clip(lists_ref[leaf, entry] - first_leaf, 0, 3 * leaves - 1) for entry in range(1, near)
            ]
            weights = jnp.concatenate([weight_ref[source] for source in sources], axis=1)
            for begin in range(0, leaf_size, tile):
                columns = pl.ds(pl.multiple_of(leaf * leaf_size + begin, tile), tile)
                kernel, slope = products(
                    [factor_ref[source] for source in sources], weights, target_ref[leaf, :, begin : begin + tile]
                )
                kernel_ref[:, columns] += kernel
                slope_ref[:, columns] += slope

    done = 0
    for step in range(1, length):
        upto = min(leaves - 1, max(done, step * (leaves - 1) // length + 1))
        if upto > done:
            run_leaves(done, upto)
            done = upto
        arrived_along(step)
        arrived_across(step - 1)
    run_leaves(done, leaves)
    arrived_across(length - 1)

    own.wait()
    for present, copies in ((has_next, to_next), (has_prev, to_prev)):

        @pl.when(present)
        def _(copies=copies):
            for copy in copies:
                copy.wait_send()

    for step in range(length):
        for present, there, copy in (
            (has_high, place - step >= 0, up(step)), (has_low, place + step < length, down(step)),
        ):

            @pl.when(jnp.logical_and(present, there))
            def _(copy=copy):
                copy.wait_send()

    for place_of in range(length):
        over(place_of).wait_send()
        for row_of in range(2):
            share(place_of, row_of).wait_send()
            remote(
                payload_ref, slot(place_of, row_of * 2 + 1 - core), core_send.at[place_of, row_of],
                core_recv.at[place_of, row_of], sibling,
            ).wait_recv()


def far_kernel(
    lists_ref, points_ref, near_kernel_ref, near_slope_ref, everything_ref,
    kernel_ref, slope_ref, block_ref, semaphore,
):
    leaves, far = lists_ref.shape
    leaf_size = points_ref.shape[1] // leaves
    tile = leaf_size // 2
    rows = block_ref.shape[2]
    dim = points_ref.shape[0]
    rhs = kernel_ref.shape[0]

    def fetch(leaf, slot):
        return pltpu.make_async_copy(
            everything_ref.at[lists_ref[leaf, slot]], block_ref.at[leaf, slot], semaphore.at[leaf, slot]
        )

    @pl.loop(0, leaves)
    def _(leaf):
        @pl.loop(0, far)
        def _(slot):
            fetch(leaf, slot).start()

    @pl.loop(0, leaves)
    def _(leaf):
        columns = pl.ds(pl.multiple_of(leaf * leaf_size, leaf_size), leaf_size)
        targets = target_factor(points_ref[:, columns].astype(jnp.float32))
        factors, halves = [], []
        for entry in range(far):
            fetch(leaf, entry).wait()
        for entry in range(far):
            for part in range(2):
                halves.append(block_ref[leaf, entry, part * rhs : (part + 1) * rhs])
            both = block_ref[leaf, entry, 2 * rhs : rows].astype(jnp.float32)
            factors.append(source_factor(jnp.concatenate([both[:dim], both[dim:]], axis=1)))
        weights = jnp.concatenate(halves, axis=1)
        for begin in range(0, leaf_size, tile):
            columns = pl.ds(pl.multiple_of(leaf * leaf_size + begin, tile), tile)
            kernel, slope = products(factors, weights, targets[:, begin : begin + tile])
            kernel_ref[:, columns] = amplitude * (near_kernel_ref[:, columns] + kernel)
            slope_ref[:, columns] = (amplitude / (length_sq * rate)) * (near_slope_ref[:, columns] + slope)


def local(points, weights, interpolation, skeleton, near_lists, far_lists):
    count = lax.axis_size("leaf")
    leaves, leaf_size, rank = interpolation.shape
    dim, rhs = points.shape[0], weights.shape[0]
    far, near = far_lists.shape[1], near_lists.shape[1]
    width = points.shape[1]
    vmem = pl.BlockSpec(memory_space=pltpu.VMEM)
    smem = pl.BlockSpec(memory_space=pltpu.SMEM)
    rows = 2 * (rhs + dim)

    def cost(sources):
        pairs = leaves * leaf_size * sources
        return pl.CostEstimate(
            flops=pairs * 2 * (256 + 512), bytes_accessed=6 * rhs * width * 2, transcendentals=pairs
        )

    partial = jax.ShapeDtypeStruct((rhs, width), jnp.float32)
    dma = pltpu.SemaphoreType.DMA
    length = count // 4
    near_kernel_part, near_slope_part, everything = pl.pallas_call(
        functools.partial(near_kernel, count),
        out_shape=(partial, partial, jax.ShapeDtypeStruct((count * leaves, rows, rank // 2), jnp.bfloat16)),
        in_specs=[smem, vmem, vmem, pl.BlockSpec(memory_space=pltpu.HBM), vmem],
        out_specs=(vmem, vmem, pl.BlockSpec(memory_space=pl.ANY)),
        scratch_shapes=[
            pltpu.VMEM((3 * leaves, leaf_size, 4 * dim), jnp.bfloat16),
            pltpu.VMEM((3 * leaves, rhs, leaf_size), jnp.bfloat16),
            pltpu.VMEM((leaves, 4 * dim, leaf_size), jnp.bfloat16),
            pltpu.VMEM((leaves, rows, rank // 2), jnp.bfloat16),
            pltpu.VMEM((2 * dim, width // 2), jnp.bfloat16),
            pltpu.VMEM((2, 2 * dim, width // 2), jnp.bfloat16),
            pltpu.VMEM((2, rhs, width), jnp.bfloat16),
            pltpu.VMEM((leaves, leaf_size, rank), jnp.bfloat16),
            dma(()), dma(()),
            dma((2, 2)), dma((2, 2)),
            dma((length + 1,)), dma((length + 1,)), dma((length + 1,)), dma((length + 1,)),
            dma((length,)), dma((length,)),
            dma((length, 2)), dma((length, 2)),
        ],
        compiler_params=pltpu.CompilerParams(
            collective_id=0, has_side_effects=True, vmem_limit_bytes=48 * MIB
        ),
        cost_estimate=cost(near * leaf_size),
    )(near_lists, points, weights, interpolation, skeleton)

    return pl.pallas_call(
        far_kernel,
        out_shape=(partial, partial),
        in_specs=[smem, vmem, vmem, vmem, pl.BlockSpec(memory_space=pl.ANY)],
        out_specs=(vmem, vmem),
        scratch_shapes=[
            pltpu.VMEM((leaves, far, rows, rank // 2), jnp.bfloat16),
            pltpu.SemaphoreType.DMA((leaves, far)),
        ],
        compiler_params=pltpu.CompilerParams(vmem_limit_bytes=48 * MIB),
        cost_estimate=cost(far * rank),
    )(far_lists, points, near_kernel_part, near_slope_part, everything)


def solution(mesh):
    placed = (
        P(None, ("groups", "leaf")),
        P(None, ("groups", "leaf")),
        P(("groups", "leaf"), None, None),
        P(("groups", "leaf"), None),
        P(("groups", "leaf"), None),
        P(("groups", "leaf"), None),
    )
    return jax.shard_map(
        local,
        mesh=mesh,
        in_specs=placed,
        out_specs=(P(None, ("groups", "leaf")), P(None, ("groups", "leaf"))),
        check_vma=False,
    )
```

```python
import functools

import jax
import jax.numpy as jnp
from jax import lax
from jax.experimental import pallas as pl
from jax.experimental.pallas import tpu as pltpu
from jax.sharding import PartitionSpec as P

amplitude = 0.03
length_sq = 4.0
log2_e = 1.4426950408889634
rate = -0.5 / length_sq * log2_e
MIB = 1024 * 1024


def pieces(x):
    high = x.astype(jnp.bfloat16).astype(jnp.float32)
    rest = x - high
    middle = rest.astype(jnp.bfloat16).astype(jnp.float32)
    low = (rest - middle).astype(jnp.bfloat16).astype(jnp.float32)
    return high, middle, low


def norm_rows(coords, first):
    norms = pieces(rate * jnp.sum(coords * coords, axis=0, keepdims=True))
    row = lax.broadcasted_iota(jnp.int32, coords.shape, 0)
    out = jnp.where(row < 6, 1.0, 0.0)
    for at, piece in enumerate(norms):
        out = jnp.where(row == first + at, piece, out)
    return out


def source_factor(coords):
    high, middle, low = pieces(coords * (-2.0 * rate))
    return jnp.concatenate([high, middle, low, norm_rows(coords, 0)], axis=0).T.astype(jnp.bfloat16)


def target_factor(coords):
    return jnp.concatenate([coords, coords, coords, norm_rows(coords, 3)], axis=0).astype(jnp.bfloat16)


def products(factors, weights, targets):
    kernels, slopes = [], []
    for factor in factors:
        exponent = jnp.dot(factor, targets, preferred_element_type=jnp.float32)
        kernel = jnp.exp2(exponent)
        kernels.append(kernel.astype(jnp.bfloat16))
        slopes.append((kernel * exponent).astype(jnp.bfloat16))
    return (
        jnp.dot(weights, jnp.concatenate(kernels, axis=0), preferred_element_type=jnp.float32),
        jnp.dot(weights, jnp.concatenate(slopes, axis=0), preferred_element_type=jnp.float32),
    )


def skeleton_block(points_ref, weights_ref, interpolation_ref, skeleton_ref, out_ref):
    leaves, leaf_size, rank = interpolation_ref.shape
    half = rank // 2
    rhs = weights_ref.shape[0]
    dim = points_ref.shape[0]
    for leaf in range(leaves):
        columns = pl.ds(leaf * leaf_size, leaf_size)
        projected = jnp.dot(
            weights_ref[:, columns], interpolation_ref[leaf], preferred_element_type=jnp.float32
        ).astype(jnp.bfloat16)
        position = lax.broadcasted_iota(jnp.int32, (leaf_size, rank), 0)
        selector = jnp.where(position == skeleton_ref[leaf : leaf + 1, :], 1.0, 0.0).astype(jnp.bfloat16)
        chosen = jnp.dot(points_ref[:, columns], selector, preferred_element_type=jnp.float32)
        out_ref[leaf, 0:rhs] = projected[:, :half]
        out_ref[leaf, rhs : 2 * rhs] = projected[:, half:]
        both = jnp.concatenate([chosen[:, :half], chosen[:, half:]], axis=0)
        out_ref[leaf, 2 * rhs : 2 * rhs + 2 * dim] = both.astype(jnp.bfloat16)


def near_kernel(
    count, lists_ref, points_ref, weights_ref, interpolation_ref, skeleton_ref,
    kernel_ref, slope_ref, all_ref,
    factor_ref, weight_ref, target_ref,
    payload_ref, packed_ref, halo_points, halo_weights, weights_vmem, skeleton_vmem, interpolation_vmem,
    own_sem, load_sem, halo_send, halo_recv, up_send, up_recv, down_send, down_recv,
    across_send, across_recv, core_send, core_recv,
):
    leaves, near = lists_ref.shape
    leaf_size = factor_ref.shape[1]
    tile = leaf_size // 2
    first_leaf = (lax.axis_index("leaf") - 1) * leaves
    dim = points_ref.shape[0]
    middle = packed_ref.shape[1]
    me = lax.axis_index("leaf")
    length = count // 4
    place, lane = me // 4, lax.rem(me, 4)
    row, core = lane // 2, lax.rem(lane, 2)
    across = place * 4 + (1 - row) * 2 + core
    sibling = place * 4 + row * 2 + (1 - core)
    has_prev, has_next = me > 0, me < count - 1
    has_low, has_high = place > 0, place < length - 1

    def remote(source, target, send, recv, device):
        return pltpu.make_async_remote_copy(
            src_ref=source, dst_ref=target, send_sem=send, recv_sem=recv,
            device_id={"leaf": device}, device_id_type=pl.DeviceIdType.MESH,
        )

    loads = [
        pltpu.make_async_copy(source, target, load_sem.at[at])
        for at, (source, target) in enumerate(
            ((weights_ref, weights_vmem), (skeleton_ref, skeleton_vmem), (interpolation_ref, interpolation_vmem))
        )
    ]
    for load in loads:
        load.start()
    barrier = pltpu.get_barrier_semaphore()

    def greet(device):
        pl.semaphore_signal(barrier, inc=1, device_id={"leaf": device}, device_id_type=pl.DeviceIdType.MESH)

    greet(across)
    greet(sibling)
    others = (
        (jnp.logical_and(has_prev, core == 0), me - 1), (jnp.logical_and(has_next, core == 1), me + 1),
        (has_low, me - 4), (has_high, me + 4),
    )
    peers = 2
    for present, device in others:
        peers = peers + present.astype(jnp.int32)

        @pl.when(present)
        def _(device=device):
            greet(device)

    packed_ref[...] = jnp.concatenate(
        [points_ref[:, :middle].astype(jnp.float32), points_ref[:, middle:].astype(jnp.float32)], axis=0
    ).astype(jnp.bfloat16)
    pl.semaphore_wait(barrier, peers)

    def halo(side, device):
        return (
            remote(packed_ref, halo_points.at[side], halo_send.at[side, 0], halo_recv.at[side, 0], device),
            remote(weights_ref, halo_weights.at[side], halo_send.at[side, 1], halo_recv.at[side, 1], device),
        )

    to_next, to_prev = halo(0, me + 1), halo(1, me - 1)
    for present, copies in ((has_next, to_next), (has_prev, to_prev)):

        @pl.when(present)
        def _(copies=copies):
            for copy in copies:
                copy.start()

    for present, side in ((has_prev, 0), (has_next, 1)):

        @pl.when(jnp.logical_not(present))
        def _(side=side):
            halo_points[side] = jnp.zeros_like(halo_points[side])
            halo_weights[side] = jnp.zeros_like(halo_weights[side])

    for load in loads:
        load.wait()
    skeleton_block(points_ref, weights_vmem, interpolation_vmem, skeleton_vmem, payload_ref)

    def slot(place_of, lane_of):
        return all_ref.at[pl.ds((place_of * 4 + lane_of) * leaves, leaves)]

    def up(step):
        source = payload_ref if step == 0 else slot(place - step, lane)
        return remote(source, slot(place - step, lane), up_send.at[step], up_recv.at[step + 1], me + 4)

    def down(step):
        source = payload_ref if step == 0 else slot(place + step, lane)
        return remote(source, slot(place + step, lane), down_send.at[step], down_recv.at[step + 1], me - 4)

    def over(place_of, source=None):
        block = slot(place_of, lane)
        return remote(
            block if source is None else source, block, across_send.at[place_of], across_recv.at[place_of], across
        )

    def share(place_of, row_of, source=None):
        block = slot(place_of, row_of * 2 + core)
        return remote(
            block if source is None else source, block,
            core_send.at[place_of, row_of], core_recv.at[place_of, row_of], sibling,
        )

    own = pltpu.make_async_copy(payload_ref, slot(place, lane), own_sem)
    own.start()
    over(place, payload_ref).start()
    share(place, row, payload_ref).start()
    for present, first in ((has_high, up(0)), (has_low, down(0))):

        @pl.when(present)
        def _(first=first):
            first.start()

    def arrived_along(step):
        @pl.when(place - step >= 0)
        def _():
            remote(payload_ref, slot(place - step, lane), up_send.at[0], up_recv.at[step], me + 4).wait_recv()

            @pl.when(has_high)
            def _():
                up(step).start()

            over(place - step).start()
            share(place - step, row).start()

        @pl.when(place + step < length)
        def _():
            remote(payload_ref, slot(place + step, lane), down_send.at[0], down_recv.at[step], me - 4).wait_recv()

            @pl.when(has_low)
            def _():
                down(step).start()

            over(place + step).start()
            share(place + step, row).start()

    def arrived_across(step):
        def one(place_of):
            remote(
                payload_ref, slot(place_of, (1 - row) * 2 + core), across_send.at[place_of],
                across_recv.at[place_of], across,
            ).wait_recv()
            share(place_of, 1 - row).start()

        if step == 0:
            one(place)
            return

        @pl.when(place - step >= 0)
        def _():
            one(place - step)

        @pl.when(place + step < length)
        def _():
            one(place + step)

    @pl.loop(0, leaves)
    def _(leaf):
        columns = pl.ds(pl.multiple_of(leaf * leaf_size, leaf_size), leaf_size)
        coords = points_ref[:, columns].astype(jnp.float32)
        factor_ref[leaves + leaf] = source_factor(coords)
        weight_ref[leaves + leaf] = weights_vmem[:, columns]
        target_ref[leaf] = target_factor(coords)
        kernel_ref[:, columns], slope_ref[:, columns] = products(
            [factor_ref[leaves + leaf]], weight_ref[leaves + leaf], target_ref[leaf]
        )

    for present, copies in ((has_prev, halo(0, me + 1)), (has_next, halo(1, me - 1))):

        @pl.when(present)
        def _(copies=copies):
            for copy in copies:
                copy.wait_recv()

    for side in range(2):
        for leaf in range(leaves):
            begin = leaf * leaf_size
            part, begin_in = begin // middle, begin % middle
            both = halo_points[side, :, begin_in : begin_in + leaf_size].astype(jnp.float32)
            coords = both[part * dim : (part + 1) * dim]
            factor_ref[2 * leaves * side + leaf] = source_factor(coords)
            weight_ref[2 * leaves * side + leaf] = halo_weights[side, :, begin : begin + leaf_size]

    def run_leaves(first, last):
        @pl.loop(first, last)
        def _(leaf):
            sources = [
                jnp.clip(lists_ref[leaf, entry] - first_leaf, 0, 3 * leaves - 1) for entry in range(1, near)
            ]
            weights = jnp.concatenate([weight_ref[source] for source in sources], axis=1)
            for begin in range(0, leaf_size, tile):
                columns = pl.ds(pl.multiple_of(leaf * leaf_size + begin, tile), tile)
                kernel, slope = products(
                    [factor_ref[source] for source in sources], weights, target_ref[leaf, :, begin : begin + tile]
                )
                kernel_ref[:, columns] += kernel
                slope_ref[:, columns] += slope

    done = 0
    for step in range(1, length):
        upto = min(leaves - 1, max(done, step * (leaves - 1) // length + 1))
        if upto > done:
            run_leaves(done, upto)
            done = upto
        arrived_along(step)
        arrived_across(step - 1)
    run_leaves(done, leaves)
    arrived_across(length - 1)

    own.wait()
    for present, copies in ((has_next, to_next), (has_prev, to_prev)):

        @pl.when(present)
        def _(copies=copies):
            for copy in copies:
                copy.wait_send()

    for step in range(length):
        for present, there, copy in (
            (has_high, place - step >= 0, up(step)), (has_low, place + step < length, down(step)),
        ):

            @pl.when(jnp.logical_and(present, there))
            def _(copy=copy):
                copy.wait_send()

    for place_of in range(length):
        over(place_of).wait_send()
        for row_of in range(2):
            share(place_of, row_of).wait_send()
            remote(
                payload_ref, slot(place_of, row_of * 2 + 1 - core), core_send.at[place_of, row_of],
                core_recv.at[place_of, row_of], sibling,
            ).wait_recv()


def far_kernel(
    lists_ref, points_ref, near_kernel_ref, near_slope_ref, everything_ref,
    kernel_ref, slope_ref, block_ref, semaphore,
):
    leaves, far = lists_ref.shape
    leaf_size = points_ref.shape[1] // leaves
    tile = leaf_size // 2
    rows = block_ref.shape[2]
    dim = points_ref.shape[0]
    rhs = kernel_ref.shape[0]

    def fetch(leaf, slot):
        return pltpu.make_async_copy(
            everything_ref.at[lists_ref[leaf, slot]], block_ref.at[leaf, slot], semaphore.at[leaf, slot]
        )

    for entry in range(far):
        fetch(0, entry).start()

    @pl.loop(0, leaves)
    def _(leaf):
        columns = pl.ds(pl.multiple_of(leaf * leaf_size, leaf_size), leaf_size)
        targets = target_factor(points_ref[:, columns].astype(jnp.float32))
        factors, halves = [], []

        @pl.when(leaf + 1 < leaves)
        def _():
            for entry in range(far):
                fetch(leaf + 1, entry).start()

        for entry in range(far):
            fetch(leaf, entry).wait()
        for entry in range(far):
            for part in range(2):
                halves.append(block_ref[leaf, entry, part * rhs : (part + 1) * rhs])
            both = block_ref[leaf, entry, 2 * rhs : rows].astype(jnp.float32)
            factors.append(source_factor(jnp.concatenate([both[:dim], both[dim:]], axis=1)))
        weights = jnp.concatenate(halves, axis=1)
        for begin in range(0, leaf_size, tile):
            columns = pl.ds(pl.multiple_of(leaf * leaf_size + begin, tile), tile)
            kernel, slope = products(factors, weights, targets[:, begin : begin + tile])
            kernel_ref[:, columns] = amplitude * (near_kernel_ref[:, columns] + kernel)
            slope_ref[:, columns] = (amplitude / (length_sq * rate)) * (near_slope_ref[:, columns] + slope)


def local(points, weights, interpolation, skeleton, near_lists, far_lists):
    count = lax.axis_size("leaf")
    leaves, leaf_size, rank = interpolation.shape
    dim, rhs = points.shape[0], weights.shape[0]
    far, near = far_lists.shape[1], near_lists.shape[1]
    width = points.shape[1]
    vmem = pl.BlockSpec(memory_space=pltpu.VMEM)
    smem = pl.BlockSpec(memory_space=pltpu.SMEM)
    rows = 2 * (rhs + dim)

    def cost(sources):
        pairs = leaves * leaf_size * sources
        return pl.CostEstimate(
            flops=pairs * 2 * (256 + 512), bytes_accessed=6 * rhs * width * 2, transcendentals=pairs
        )

    partial = jax.ShapeDtypeStruct((rhs, width), jnp.float32)
    dma = pltpu.SemaphoreType.DMA
    length = count // 4
    near_kernel_part, near_slope_part, everything = pl.pallas_call(
        functools.partial(near_kernel, count),
        out_shape=(partial, partial, jax.ShapeDtypeStruct((count * leaves, rows, rank // 2), jnp.bfloat16)),
        in_specs=[smem, vmem] + [pl.BlockSpec(memory_space=pltpu.HBM)] * 3,
        out_specs=(vmem, vmem, pl.BlockSpec(memory_space=pl.ANY)),
        scratch_shapes=[
            pltpu.VMEM((3 * leaves, leaf_size, 4 * dim), jnp.bfloat16),
            pltpu.VMEM((3 * leaves, rhs, leaf_size), jnp.bfloat16),
            pltpu.VMEM((leaves, 4 * dim, leaf_size), jnp.bfloat16),
            pltpu.VMEM((leaves, rows, rank // 2), jnp.bfloat16),
            pltpu.VMEM((2 * dim, width // 2), jnp.bfloat16),
            pltpu.VMEM((2, 2 * dim, width // 2), jnp.bfloat16),
            pltpu.VMEM((2, rhs, width), jnp.bfloat16),
            pltpu.VMEM((rhs, width), jnp.bfloat16),
            pltpu.VMEM((leaves, rank), jnp.int32),
            pltpu.VMEM((leaves, leaf_size, rank), jnp.bfloat16),
            dma(()), dma((3,)),
            dma((2, 2)), dma((2, 2)),
            dma((length + 1,)), dma((length + 1,)), dma((length + 1,)), dma((length + 1,)),
            dma((length,)), dma((length,)),
            dma((length, 2)), dma((length, 2)),
        ],
        compiler_params=pltpu.CompilerParams(
            collective_id=0, has_side_effects=True, vmem_limit_bytes=48 * MIB
        ),
        cost_estimate=cost(near * leaf_size),
    )(near_lists, points, weights, interpolation, skeleton)

    return pl.pallas_call(
        far_kernel,
        out_shape=(partial, partial),
        in_specs=[smem, vmem, vmem, vmem, pl.BlockSpec(memory_space=pl.ANY)],
        out_specs=(vmem, vmem),
        scratch_shapes=[
            pltpu.VMEM((leaves, far, rows, rank // 2), jnp.bfloat16),
            pltpu.SemaphoreType.DMA((leaves, far)),
        ],
        compiler_params=pltpu.CompilerParams(vmem_limit_bytes=48 * MIB),
        cost_estimate=cost(far * rank),
    )(far_lists, points, near_kernel_part, near_slope_part, everything)


def solution(mesh):
    placed = (
        P(None, ("groups", "leaf")),
        P(None, ("groups", "leaf")),
        P(("groups", "leaf"), None, None),
        P(("groups", "leaf"), None),
        P(("groups", "leaf"), None),
        P(("groups", "leaf"), None),
    )
    return jax.shard_map(
        local,
        mesh=mesh,
        in_specs=placed,
        out_specs=(P(None, ("groups", "leaf")), P(None, ("groups", "leaf"))),
        check_vma=False,
    )
```
